32 devices in a mesh: groups: 2 (over x), inst: 16 (over z, y, core).
Axes of the slice: x: 2, y: 2, z: 4, core: 2. Of those that a mesh axis runs over, the one named last changes fastest.
Arguments:
- queries: bfloat16 [4096, 8192], P(('groups', 'inst')), parts along dimension 0, may hold values from -128 to 128
- span_kv: bfloat16 [4096, 2048], P(('groups', 'inst')), parts along dimension 0, may hold values from -6 to 6
- prefix_kv: bfloat16 [32768, 2048], P(('groups', 'inst')), parts along dimension 0, may hold values from -6 to 6
- span_counts: int32 [32], P('groups'), parts along dimension 0, may hold values from 1 to 128, 1536 in all
- prefix_lengths: int32 [32], P('groups'), parts along dimension 0, may hold values from 1 to 1024, 10240 in all
- move_to: int32 [32], P('groups'), parts along dimension 0, may hold values from 0 to 15, each once
- page_slot: int32 [256], P('groups'), parts along dimension 0, may hold values from 0 to 127, each once
Outputs:
- attn_out: bfloat16 [4096, 8192], P(('groups', 'inst')), parts along dimension 0
- decode_pages: bfloat16 [256, 16, 2048], P(('groups', 'inst')), parts along dimension 0
The draws below stay inside these ranges and needn't reach their ends.
There are 2 independent parts, one for each index of `groups`. The reference program is written for one: setup_inputs(seed, part) draws one part's arguments, and reference() takes and returns one part's arrays. A program takes and returns all parts, laid end to end along the dimension named above; each array names one. Nothing has to cross between parts.
Inputs may be any that keep to these rules, and one draw needn't show every extreme that they name: `move_to`: each instance's span result goes to exactly one instance, and each instance receives exactly one. `page_slot`: each decode slot receives exactly one page.
All inputs are finite; a program needn't handle non-finite values.
Results may differ from the reference program's by a relative error of at most 0.0049.
Values may be sent and summed in bfloat16 or wider, within the bound.
A program may use at most 64 MiB of HBM per device.

```python
import math
import jax
import jax.numpy as jnp
import numpy as np
from jax import lax

HEADS = 64
KV_HEADS = 8
HEAD_DIM = 128
SPAN = 128
PREFIX = 1024
PAGE = 16
PAGES_DEV = 8
N_INST = 16


def draw_queries(key, part):
    key = jax.random.fold_in(key, 5)
    shape = (N_INST, SPAN, HEADS, HEAD_DIM)
    base = jax.random.truncated_normal(key, -6.0, 6.0, shape, jnp.float32)
    return base.reshape(N_INST * SPAN, HEADS * HEAD_DIM).astype(jnp.bfloat16)


def draw_span_kv(key, part):
    key = jax.random.fold_in(key, 7)
    key_width = KV_HEADS * HEAD_DIM
    shape = (N_INST, SPAN, 2 * key_width)
    base = jax.random.truncated_normal(key, -6.0, 6.0, shape, jnp.float32)
    return base.reshape(N_INST * SPAN, 2 * key_width).astype(jnp.bfloat16)


def draw_prefix_kv(key, part):
    key = jax.random.fold_in(key, 11)
    key_width = KV_HEADS * HEAD_DIM
    shape = (N_INST, PREFIX, 2 * key_width)
    base = jax.random.truncated_normal(key, -6.0, 6.0, shape, jnp.float32)
    return base.reshape(N_INST * PREFIX, 2 * key_width).astype(jnp.bfloat16)


def split_up(count, total, bound, slope):
    loads = [(1 << 20) // math.isqrt(rank ** slope) + 1 for rank in range(2, count + 1)]
    rest, holding = total - bound - (count - 1), [1] * (count - 1)
    while rest > 0:
        candidates = [i for i in range(count - 1) if holding[i] < bound]
        whole, budget = sum([loads[i] for i in candidates]), rest
        for i in candidates:
            addition = min(bound - holding[i], max(1, budget * loads[i] // whole), rest)
            holding[i] = holding[i] + addition
            rest = rest - addition
    return np.array([bound] + holding)


def ragged_sizes(own_key, number_of, total, limit, skew):
    if number_of == 2:
        one = jax.random.randint(own_key, (), max(1, total - limit), min(limit, total - 1) + 1)
        return jnp.stack([one, total - one])
    lengths = jnp.asarray(split_up(number_of, total, limit, skew), jnp.int32)
    twos = (number_of - 1) // 2
    source_of, receiver = lengths[1:1 + 2 * twos:2], lengths[2:2 + 2 * twos:2]
    margin = jnp.minimum(source_of - 1, limit - receiver)
    moved = jax.random.randint(jax.random.fold_in(own_key, 1), (twos,), 0, 1 << 20) % (margin + 1)
    lengths = lengths.at[1:1 + 2 * twos:2].set(source_of - moved).at[2:2 + 2 * twos:2].set(receiver + moved)
    return lengths[jax.random.permutation(jax.random.fold_in(own_key, 2), number_of)]


def setup_inputs(seed: int = 0, part: int = 0) -> dict:
    arg_keys = jax.random.split(jax.random.key(seed), 8)
    part_keys = jax.random.split(jax.random.fold_in(arg_keys[7], part), 8)
    queries = draw_queries(jax.random.fold_in(jax.random.fold_in(arg_keys[7], part), 71), part)
    span_kv = draw_span_kv(jax.random.fold_in(jax.random.fold_in(arg_keys[7], part), 71), part)
    prefix_kv = draw_prefix_kv(jax.random.fold_in(jax.random.fold_in(arg_keys[7], part), 71), part)
    span_counts = ragged_sizes(part_keys[3], N_INST, N_INST * SPAN * 3 // 4, SPAN, 2).astype(jnp.int32)
    prefix_lengths = ragged_sizes(part_keys[4], N_INST, N_INST * PREFIX * 5 // 8, PREFIX, 2).astype(jnp.int32)
    move_to = jax.random.permutation(part_keys[5], N_INST).astype(jnp.int32)
    page_slot = jax.random.permutation(part_keys[6], N_INST * PAGES_DEV).astype(jnp.int32)
    return dict(queries=queries, span_kv=span_kv, prefix_kv=prefix_kv, span_counts=span_counts, prefix_lengths=prefix_lengths, move_to=move_to, page_slot=page_slot)


def attend(queries, span_kv, prefix_kv, live_rows, length):
    row_count = queries.shape[0]
    prefix = prefix_kv.shape[0]
    key_width = KV_HEADS * HEAD_DIM
    per_group = HEADS // KV_HEADS
    keys_all = jnp.concatenate([prefix_kv[:, :key_width], span_kv[:, :key_width]], axis=0)
    values_all = jnp.concatenate([prefix_kv[:, key_width:], span_kv[:, key_width:]], axis=0)
    position = jnp.arange(row_count * per_group, dtype=jnp.int32) // per_group
    column = jnp.arange(prefix + row_count, dtype=jnp.int32)
    visible = jnp.where(column[None, :] < prefix, column[None, :] < length, column[None, :] - prefix <= position[:, None])
    score_scale = 1.0 / math.sqrt(HEAD_DIM)
    pieces = []
    for kv_head in range(KV_HEADS):
        width = per_group * HEAD_DIM
        query_rows = queries[:, kv_head * width:(kv_head + 1) * width].reshape(row_count * per_group, HEAD_DIM)
        key_block = keys_all[:, kv_head * HEAD_DIM:(kv_head + 1) * HEAD_DIM]
        value_block = values_all[:, kv_head * HEAD_DIM:(kv_head + 1) * HEAD_DIM]
        scores = lax.dot_general(query_rows, key_block, (((1,), (1,)), ((), ())), preferred_element_type=jnp.float32) * score_scale
        scores = jnp.where(visible, scores, -jnp.inf)
        row_max = lax.optimization_barrier(jnp.max(scores, axis=1, keepdims=True))
        shifted = jnp.exp(scores - row_max)
        weights = (shifted / lax.optimization_barrier(jnp.sum(shifted, axis=1, keepdims=True))).astype(jnp.bfloat16)
        mixed = jnp.dot(weights, value_block, preferred_element_type=jnp.float32)
        pieces.append(mixed.reshape(row_count, width))
    result = jnp.concatenate(pieces, axis=1)
    active = jnp.arange(row_count, dtype=jnp.int32) < live_rows
    return jnp.where(active[:, None], result, 0.0).astype(jnp.bfloat16)

def reference(queries, span_kv, prefix_kv, span_counts, prefix_lengths, move_to, page_slot):
    query_blocks = queries.reshape(N_INST, SPAN, HEADS * HEAD_DIM)
    span_blocks = span_kv.reshape(N_INST, SPAN, 2 * KV_HEADS * HEAD_DIM)
    prefix_blocks = prefix_kv.reshape(N_INST, PREFIX, 2 * KV_HEADS * HEAD_DIM)

    def one_instance(items):
        return attend(items[0], items[1], items[2], items[3], items[4])
    outputs = lax.map(one_instance, (query_blocks, span_blocks, prefix_blocks, span_counts, prefix_lengths))
    placed = jnp.zeros_like(outputs).at[move_to].set(outputs)
    attn_out = placed.reshape(N_INST * SPAN, HEADS * HEAD_DIM)
    pages = span_kv.reshape(N_INST * PAGES_DEV, PAGE, 2 * KV_HEADS * HEAD_DIM)
    decode_pages = jnp.zeros_like(pages).at[page_slot].set(pages)
    return (attn_out, decode_pages)
```

```python
import functools
import math

import jax
import jax.numpy as jnp
from jax import lax
from jax.experimental import pallas as pl
from jax.experimental.pallas import tpu as pltpu
from jax.sharding import PartitionSpec as P

HEADS = 64
KV_HEADS = 8
HEAD_DIM = 128
PAGE = 16
KEY_WIDTH = KV_HEADS * HEAD_DIM
GROUP_WIDTH = HEADS // KV_HEADS * HEAD_DIM
ROWS = 16
COLS = 512
MESH = pl.DeviceIdType.MESH


def kernel(n, with_pages, *refs):
    if with_pages:
        (counts, lengths, source_of, page_source, q_hbm, span_hbm, prefix_hbm, new_hbm,
         out_hbm, pages_hbm, q, kv, bias, stage, relay, *rest) = refs
        chunks = 128 // n
        held = rest[:chunks]
        (page_stage, page_held, q_sem, k_sem, v_sem, span_sem, send_sem, held_sem, relay_sem,
         out_sem, page_sem) = rest[chunks:]
    else:
        (counts, lengths, source_of, q_hbm, span_hbm, prefix_hbm,
         out_hbm, q, kv, bias, stage, relay, *rest) = refs
        chunks = 128 // n
        held = rest[:chunks]
        q_sem, k_sem, v_sem, span_sem, send_sem, held_sem, relay_sem, out_sem = rest[chunks:]
    me = lax.axis_index("inst")
    span = span_hbm.shape[0]
    prefix = prefix_hbm.shape[0]
    keys = prefix + span

    span_copies = [
        pltpu.make_async_copy(span_hbm, kv.at[pl.ds(prefix, span)], span_sem)
    ]
    loads = []
    for g in range(KV_HEADS):
        wide = pl.ds(g * GROUP_WIDTH, GROUP_WIDTH)
        k_cols = pl.ds(g * HEAD_DIM, HEAD_DIM)
        v_cols = pl.ds(KEY_WIDTH + g * HEAD_DIM, HEAD_DIM)
        loads.append([
            pltpu.make_async_copy(q_hbm.at[:, wide], q.at[:, wide], q_sem.at[g]),
            pltpu.make_async_copy(
                prefix_hbm.at[:, k_cols], kv.at[pl.ds(0, prefix), k_cols], k_sem.at[g]),
            pltpu.make_async_copy(
                prefix_hbm.at[:, v_cols], kv.at[pl.ds(0, prefix), v_cols], v_sem.at[g]),
        ])
    span_copies[0].start()
    for group in loads:
        for copy in group:
            copy.start()

    barrier = pltpu.get_barrier_semaphore()

    @pl.loop(1, n)
    def _(k):
        pl.semaphore_signal(
            barrier, inc=1, device_id={"inst": lax.rem(me + k, n)}, device_id_type=MESH)

    count = counts[me]
    length = lengths[me]
    row = lax.broadcasted_iota(jnp.int32, (span, keys), 0)
    column = lax.broadcasted_iota(jnp.int32, (span, keys), 1)
    limit = jnp.where(column < prefix, length, row + (prefix + 1))
    bias[...] = jnp.where(column < limit, 0.0, -1e30)
    pl.semaphore_wait(barrier, n - 1)

    if with_pages:
        pages_dev = span // PAGE

        @pl.loop(1, n)
        def _(k):
            peer = lax.rem(me + k, n)
            pltpu.make_async_remote_copy(
                src_ref=new_hbm.at[:, :, pl.ds(pl.multiple_of(peer * 128, 128), 128)],
                dst_ref=page_held.at[pl.ds(me * pages_dev, pages_dev)],
                send_sem=page_sem.at[0],
                recv_sem=page_sem.at[1],
                device_id={"inst": peer},
                device_id_type=MESH,
            ).start()

        pltpu.make_async_copy(
            new_hbm.at[:, :, pl.ds(pl.multiple_of(me * 128, 128), 128)],
            page_held.at[pl.ds(me * pages_dev, pages_dev)],
            page_sem.at[1],
        ).start()

    scale = math.log2(math.e) / math.sqrt(HEAD_DIM)
    live = lax.broadcasted_iota(jnp.int32, (span, HEAD_DIM), 0) < count

    def attend(g):
        @pl.loop(0, 4)
        def _(pair):
            first = pl.multiple_of(g * GROUP_WIDTH + pair * 256, 256)
            two = q[:, pl.ds(first, 256)]
            rows = jnp.concatenate([two[:, :HEAD_DIM], two[:, HEAD_DIM:]], axis=0)
            key = kv[:, g * HEAD_DIM:(g + 1) * HEAD_DIM]
            value = kv[:, KEY_WIDTH + g * HEAD_DIM:KEY_WIDTH + (g + 1) * HEAD_DIM]
            scores = lax.dot_general(
                rows, key, (((1,), (1,)), ((), ())), preferred_element_type=jnp.float32)
            scores = scores.reshape(2, span, keys) * scale + bias[...][None]
            top = jnp.max(scores, axis=2, keepdims=True)
            shifted = jnp.exp2(scores - top)
            total = jnp.sum(shifted, axis=2, keepdims=True)
            mixed = jnp.dot(
                shifted.reshape(2 * span, keys).astype(jnp.bfloat16), value,
                preferred_element_type=jnp.float32)
            mixed = mixed.reshape(2, span, HEAD_DIM) / total
            mixed = jnp.where(live[None], mixed, 0.0).astype(jnp.bfloat16)
            half = pair // 2
            for h in range(2):
                at = pl.multiple_of((pair % 2) * 256 + h * HEAD_DIM, HEAD_DIM)
                for r in range(8):
                    stage[g, half * 8 + r, :, pl.ds(at, HEAD_DIM)] = (
                        mixed[h, r * ROWS:(r + 1) * ROWS])

    def spread(g):
        c = g * 16 // n

        @pl.loop(0, 16)
        def _(k):
            j = lax.rem(me + k, 16)
            target = (g * 16) % n + j

            @pl.when(target != me)
            def _():
                pltpu.make_async_remote_copy(
                    src_ref=stage.at[g, j],
                    dst_ref=held[c].at[me],
                    send_sem=send_sem.at[0],
                    recv_sem=held_sem.at[c],
                    device_id={"inst": target},
                    device_id_type=MESH,
                ).start()

            @pl.when(target == me)
            def _():
                pltpu.make_async_copy(stage.at[g, j], held[c].at[me], held_sem.at[c]).start()

    def send_on(c):
        pltpu.make_async_copy(held[c], held[c], held_sem.at[c]).wait()
        piece = c * n + me
        g = piece // 16
        j = piece % 16
        place = out_hbm.at[
            pl.ds(pl.multiple_of((j % 8) * ROWS, ROWS), ROWS),
            pl.ds(pl.multiple_of(g * GROUP_WIDTH + (j // 8) * COLS, COLS), COLS),
        ]

        @pl.loop(0, n)
        def _(k):
            peer = lax.rem(me + k, n)
            relay[c, peer] = held[c][source_of[peer]]

            @pl.when(k > 0)
            def _():
                pltpu.make_async_remote_copy(
                    src_ref=relay.at[c, peer],
                    dst_ref=place,
                    send_sem=relay_sem.at[0],
                    recv_sem=out_sem.at[0],
                    device_id={"inst": peer},
                    device_id_type=MESH,
                ).start()

            @pl.when(k == 0)
            def _():
                pltpu.make_async_copy(relay.at[c, peer], place, out_sem.at[0]).start()

    def send_pages():
        pltpu.make_async_copy(page_held, page_held, page_sem.at[1]).wait()
        place = pages_hbm.at[:, :, pl.ds(pl.multiple_of(me * 128, 128), 128)]

        @pl.loop(0, n)
        def _(k):
            peer = lax.rem(me + k, n)
            for slot in range(pages_dev):
                at = peer * pages_dev + slot
                page_stage[at] = page_held[page_source[at]]

            src = page_stage.at[pl.ds(peer * pages_dev, pages_dev)]

            @pl.when(k > 0)
            def _():
                pltpu.make_async_remote_copy(
                    src_ref=src,
                    dst_ref=place,
                    send_sem=page_sem.at[2],
                    recv_sem=page_sem.at[3],
                    device_id={"inst": peer},
                    device_id_type=MESH,
                ).start()

            @pl.when(k == 0)
            def _():
                pltpu.make_async_copy(src, place, page_sem.at[3]).start()

    lag = 3
    span_copies[0].wait()
    sent = 0
    for g in range(KV_HEADS):
        for copy in loads[g]:
            copy.wait()
        attend(g)
        spread(g)
        if with_pages and g == 3:
            send_pages()
        if n == 16 and g >= lag:
            send_on(sent)
            sent += 1
    for c in range(sent, chunks):
        send_on(c)

    away = 128 - chunks
    flat = stage.at[:, pl.ds(0, 15)]
    if n == 16:
        pltpu.make_async_copy(flat, flat, send_sem.at[0]).wait()
        flat = relay.at[:, pl.ds(0, n - 1)]
        pltpu.make_async_copy(flat, flat, relay_sem.at[0]).wait()
    else:
        flat = relay.at[0, pl.ds(0, away)]
        pltpu.make_async_copy(flat, flat, send_sem.at[0]).wait()
        pltpu.make_async_copy(flat, flat, relay_sem.at[0]).wait()
    pltpu.make_async_copy(out_hbm, out_hbm, out_sem.at[0]).wait()
    if with_pages:
        some = page_held.at[pl.ds(0, (n - 1) * pages_dev)]
        pltpu.make_async_copy(some, some, page_sem.at[0]).wait()
        some = page_stage.at[pl.ds(0, (n - 1) * pages_dev)]
        pltpu.make_async_copy(some, some, page_sem.at[2]).wait()
        pltpu.make_async_copy(pages_hbm, pages_hbm, page_sem.at[3]).wait()


def inverse(order):
    index = jnp.arange(order.shape[0], dtype=jnp.int32)
    return jnp.sum(jnp.where(order[None, :] == index[:, None], index[None, :], 0), axis=1)


def move_pages(span_kv, page_slot, inst_count):
    pages_here = span_kv.shape[0] // PAGE
    piece_width = PAGE * span_kv.shape[1] // inst_count
    flat_pages = span_kv.reshape(pages_here, inst_count, piece_width)
    spread_pages = lax.all_to_all(flat_pages, "inst", split_axis=1, concat_axis=0, tiled=True)
    ordered_pages = jnp.take(spread_pages, inverse(page_slot), axis=0)
    arrived = lax.all_to_all(ordered_pages, "inst", split_axis=0, concat_axis=1, tiled=True)
    return arrived.reshape(pages_here, PAGE, span_kv.shape[1])


def local(n, queries, span_kv, prefix_kv, span_counts, prefix_lengths, move_to, page_slot):
    span, width = queries.shape
    prefix, kv_width = prefix_kv.shape
    with_pages = n * 128 == kv_width
    chunks = 128 // n
    anywhere = pl.BlockSpec(memory_space=pl.ANY)
    scalars = pl.BlockSpec(memory_space=pltpu.SMEM)
    small = [span_counts, prefix_lengths, inverse(move_to)]
    out_shape = [jax.ShapeDtypeStruct((span, width), jnp.bfloat16)]
    scratch = [
        pltpu.VMEM((span, width), jnp.bfloat16),
        pltpu.VMEM((prefix + span, kv_width), jnp.bfloat16),
        pltpu.VMEM((span, prefix + span), jnp.float32),
        pltpu.VMEM((KV_HEADS, 16, ROWS, COLS), jnp.bfloat16),
        pltpu.VMEM((chunks, n, ROWS, COLS), jnp.bfloat16),
    ] + [pltpu.VMEM((n, ROWS, COLS), jnp.bfloat16) for _ in range(chunks)]
    big = [queries, span_kv, prefix_kv]
    if with_pages:
        small.append(inverse(page_slot))
        big.append(span_kv.reshape(span // PAGE, PAGE, kv_width))
        out_shape.append(jax.ShapeDtypeStruct((span // PAGE, PAGE, kv_width), jnp.bfloat16))
        scratch += [
            pltpu.VMEM((page_slot.shape[0], PAGE, 128), jnp.bfloat16),
            pltpu.VMEM((page_slot.shape[0], PAGE, 128), jnp.bfloat16),
        ]
    dma = pltpu.SemaphoreType.DMA
    scratch += [
        dma((KV_HEADS,)), dma((KV_HEADS,)), dma((KV_HEADS,)), dma(()),
        dma((1,)), dma((chunks,)), dma((1,)), dma((1,)),
    ]
    if with_pages:
        scratch.append(dma((4,)))
    outs = pl.pallas_call(
        functools.partial(kernel, n, with_pages),
        out_shape=out_shape,
        in_specs=[scalars] * len(small) + [anywhere] * len(big),
        out_specs=[anywhere] * len(out_shape),
        scratch_shapes=scratch,
        compiler_params=pltpu.CompilerParams(
            collective_id=0, has_side_effects=True, vmem_limit_bytes=48 * 1024 * 1024),
    )(*small, *big)
    if with_pages:
        return outs[0], outs[1]
    return outs[0], move_pages(span_kv, page_slot, n)


def solution(mesh):
    placed = (
        P(("groups", "inst"), None),
        P(("groups", "inst"), None),
        P(("groups", "inst"), None),
        P("groups"),
        P("groups"),
        P("groups"),
        P("groups"),
    )
    return jax.shard_map(
        functools.partial(local, mesh.shape["inst"]),
        mesh=mesh,
        in_specs=placed,
        out_specs=(P(("groups", "inst"), None), P(("groups", "inst"), None, None)),
        check_vma=False,
    )
```

```python
import functools
import math

import jax
import jax.numpy as jnp
from jax import lax
from jax.experimental import pallas as pl
from jax.experimental.pallas import tpu as pltpu
from jax.sharding import PartitionSpec as P

HEADS = 64
KV_HEADS = 8
HEAD_DIM = 128
PAGE = 16
KEY_WIDTH = KV_HEADS * HEAD_DIM
GROUP_WIDTH = HEADS // KV_HEADS * HEAD_DIM
ROWS = 16
COLS = 512
LIMITS = (5, 8)
MESH = pl.DeviceIdType.MESH


def kernel(n, with_pages, *refs):
    if with_pages:
        (counts, lengths, source_of, page_source, q_hbm, span_hbm, prefix_hbm, new_hbm,
         out_hbm, pages_hbm, q, kv, bias, stage, relay, *rest) = refs
        chunks = 128 // n
        held = rest[:chunks]
        (page_stage, page_held, q_sem, k_sem, v_sem, span_sem, send_sem, held_sem, relay_sem,
         out_sem, page_sem) = rest[chunks:]
    else:
        (counts, lengths, source_of, q_hbm, span_hbm, prefix_hbm,
         out_hbm, q, kv, bias, stage, relay, *rest) = refs
        chunks = 128 // n
        held = rest[:chunks]
        q_sem, k_sem, v_sem, span_sem, send_sem, held_sem, relay_sem, out_sem = rest[chunks:]
    me = lax.axis_index("inst")
    span = span_hbm.shape[0]
    prefix = prefix_hbm.shape[0]
    keys = prefix + span

    span_copies = [
        pltpu.make_async_copy(span_hbm, kv.at[pl.ds(prefix, span)], span_sem)
    ]
    loads = []
    for g in range(KV_HEADS):
        wide = pl.ds(g * GROUP_WIDTH, GROUP_WIDTH)
        k_cols = pl.ds(g * HEAD_DIM, HEAD_DIM)
        v_cols = pl.ds(KEY_WIDTH + g * HEAD_DIM, HEAD_DIM)
        loads.append([
            pltpu.make_async_copy(q_hbm.at[:, wide], q.at[:, wide], q_sem.at[g]),
            pltpu.make_async_copy(
                prefix_hbm.at[:, k_cols], kv.at[pl.ds(0, prefix), k_cols], k_sem.at[g]),
            pltpu.make_async_copy(
                prefix_hbm.at[:, v_cols], kv.at[pl.ds(0, prefix), v_cols], v_sem.at[g]),
        ])
    span_copies[0].start()
    for group in loads:
        for copy in group:
            copy.start()

    barrier = pltpu.get_barrier_semaphore()

    @pl.loop(1, n)
    def _(k):
        pl.semaphore_signal(
            barrier, inc=1, device_id={"inst": lax.rem(me + k, n)}, device_id_type=MESH)

    count = counts[me]
    length = lengths[me]
    row = lax.broadcasted_iota(jnp.int32, (span, keys), 0)
    column = lax.broadcasted_iota(jnp.int32, (span, keys), 1)
    limit = jnp.where(column < prefix, length, row + (prefix + 1))
    bias[...] = jnp.where(column < limit, 0.0, -1e30)
    pl.semaphore_wait(barrier, n - 1)

    if with_pages:
        pages_dev = span // PAGE

        @pl.loop(1, n)
        def _(k):
            peer = lax.rem(me + k, n)
            pltpu.make_async_remote_copy(
                src_ref=new_hbm.at[:, :, pl.ds(pl.multiple_of(peer * 128, 128), 128)],
                dst_ref=page_held.at[pl.ds(me * pages_dev, pages_dev)],
                send_sem=page_sem.at[0],
                recv_sem=page_sem.at[1],
                device_id={"inst": peer},
                device_id_type=MESH,
            ).start()

        pltpu.make_async_copy(
            new_hbm.at[:, :, pl.ds(pl.multiple_of(me * 128, 128), 128)],
            page_held.at[pl.ds(me * pages_dev, pages_dev)],
            page_sem.at[1],
        ).start()

    scale = math.log2(math.e) / math.sqrt(HEAD_DIM)
    live = lax.broadcasted_iota(jnp.int32, (span, HEAD_DIM), 0) < count

    def attend(g):
        @pl.loop(0, 4)
        def _(pair):
            first = pl.multiple_of(g * GROUP_WIDTH + pair * 256, 256)
            two = q[:, pl.ds(first, 256)]
            rows = jnp.concatenate([two[:, :HEAD_DIM], two[:, HEAD_DIM:]], axis=0)
            key = kv[:, g * HEAD_DIM:(g + 1) * HEAD_DIM]
            value = kv[:, KEY_WIDTH + g * HEAD_DIM:KEY_WIDTH + (g + 1) * HEAD_DIM]
            scores = lax.dot_general(
                rows, key, (((1,), (1,)), ((), ())), preferred_element_type=jnp.float32)
            scores = scores.reshape(2, span, keys) * scale + bias[...][None]
            top = jnp.max(scores, axis=2, keepdims=True)
            shifted = jnp.exp2(scores - top)
            total = jnp.sum(shifted, axis=2, keepdims=True)
            mixed = jnp.dot(
                shifted.reshape(2 * span, keys).astype(jnp.bfloat16), value,
                preferred_element_type=jnp.float32)
            mixed = mixed.reshape(2, span, HEAD_DIM) / total
            mixed = jnp.where(live[None], mixed, 0.0).astype(jnp.bfloat16)
            half = pair // 2
            for h in range(2):
                at = pl.multiple_of((pair % 2) * 256 + h * HEAD_DIM, HEAD_DIM)
                for r in range(8):
                    stage[g, half * 8 + r, :, pl.ds(at, HEAD_DIM)] = (
                        mixed[h, r * ROWS:(r + 1) * ROWS])

    def spread(g):
        c = g * 16 // n

        @pl.loop(0, 16)
        def _(k):
            j = lax.rem(me + k, 16)
            target = (g * 16) % n + j

            @pl.when(target != me)
            def _():
                pltpu.make_async_remote_copy(
                    src_ref=stage.at[g, j],
                    dst_ref=held[c].at[me],
                    send_sem=send_sem.at[0],
                    recv_sem=held_sem.at[c],
                    device_id={"inst": target},
                    device_id_type=MESH,
                ).start()

            @pl.when(target == me)
            def _():
                pltpu.make_async_copy(stage.at[g, j], held[c].at[me], held_sem.at[c]).start()

    def send_on(c):
        pltpu.make_async_copy(held[c], held[c], held_sem.at[c]).wait()
        piece = c * n + me
        g = piece // 16
        j = piece % 16
        place = out_hbm.at[
            pl.ds(pl.multiple_of((j % 8) * ROWS, ROWS), ROWS),
            pl.ds(pl.multiple_of(g * GROUP_WIDTH + (j // 8) * COLS, COLS), COLS),
        ]

        @pl.loop(0, n)
        def _(k):
            peer = lax.rem(me + k, n)
            relay[c, peer] = held[c][source_of[peer]]

            @pl.when(k > 0)
            def _():
                pltpu.make_async_remote_copy(
                    src_ref=relay.at[c, peer],
                    dst_ref=place,
                    send_sem=relay_sem.at[0],
                    recv_sem=out_sem.at[0],
                    device_id={"inst": peer},
                    device_id_type=MESH,
                ).start()

            @pl.when(k == 0)
            def _():
                pltpu.make_async_copy(relay.at[c, peer], place, out_sem.at[0]).start()

    def send_pages():
        pltpu.make_async_copy(page_held, page_held, page_sem.at[1]).wait()
        place = pages_hbm.at[:, :, pl.ds(pl.multiple_of(me * 128, 128), 128)]

        @pl.loop(0, n)
        def _(k):
            peer = lax.rem(me + k, n)
            for slot in range(pages_dev):
                at = peer * pages_dev + slot
                page_stage[at] = page_held[page_source[at]]

            src = page_stage.at[pl.ds(peer * pages_dev, pages_dev)]

            @pl.when(k > 0)
            def _():
                pltpu.make_async_remote_copy(
                    src_ref=src,
                    dst_ref=place,
                    send_sem=page_sem.at[2],
                    recv_sem=page_sem.at[3],
                    device_id={"inst": peer},
                    device_id_type=MESH,
                ).start()

            @pl.when(k == 0)
            def _():
                pltpu.make_async_copy(src, place, page_sem.at[3]).start()

    lag = 3
    span_copies[0].wait()
    sent = 0
    for g in range(KV_HEADS):
        for copy in loads[g]:
            copy.wait()
        attend(g)
        spread(g)
        if with_pages and g == 3:
            send_pages()
        if n == 16 and g >= lag:
            send_on(sent)
            sent += 1
    for c in range(sent, chunks):
        send_on(c)

    away = 128 - chunks
    flat = stage.at[:, pl.ds(0, 15)]
    if n == 16:
        pltpu.make_async_copy(flat, flat, send_sem.at[0]).wait()
        flat = relay.at[:, pl.ds(0, n - 1)]
        pltpu.make_async_copy(flat, flat, relay_sem.at[0]).wait()
    else:
        flat = relay.at[0, pl.ds(0, away)]
        pltpu.make_async_copy(flat, flat, send_sem.at[0]).wait()
        pltpu.make_async_copy(flat, flat, relay_sem.at[0]).wait()
    pltpu.make_async_copy(out_hbm, out_hbm, out_sem.at[0]).wait()
    if with_pages:
        some = page_held.at[pl.ds(0, (n - 1) * pages_dev)]
        pltpu.make_async_copy(some, some, page_sem.at[0]).wait()
        some = page_stage.at[pl.ds(0, (n - 1) * pages_dev)]
        pltpu.make_async_copy(some, some, page_sem.at[2]).wait()
        pltpu.make_async_copy(pages_hbm, pages_hbm, page_sem.at[3]).wait()


def inverse(order):
    index = jnp.arange(order.shape[0], dtype=jnp.int32)
    return jnp.sum(jnp.where(order[None, :] == index[:, None], index[None, :], 0), axis=1)


def move_pages(span_kv, page_slot, inst_count):
    pages_here = span_kv.shape[0] // PAGE
    piece_width = PAGE * span_kv.shape[1] // inst_count
    flat_pages = span_kv.reshape(pages_here, inst_count, piece_width)
    spread_pages = lax.all_to_all(flat_pages, "inst", split_axis=1, concat_axis=0, tiled=True)
    ordered_pages = jnp.take(spread_pages, inverse(page_slot), axis=0)
    arrived = lax.all_to_all(ordered_pages, "inst", split_axis=0, concat_axis=1, tiled=True)
    return arrived.reshape(pages_here, PAGE, span_kv.shape[1])


def line_kernel(n, most, counts, lengths, source_of, page_source, plan, q_hbm, span_hbm,
                prefix_hbm, new_hbm, out_hbm, pages_hbm, q, kv, bias, stage, middle, outward,
                final, page_stage, page_held, *rest):
    near, far = rest[:KV_HEADS], rest[KV_HEADS:2 * KV_HEADS]
    (q_sem, k_sem, v_sem, span_sem, near_sem, next_sem, far_sem, page_sem,
     sent) = rest[2 * KV_HEADS:]
    me = lax.axis_index("inst")
    plane, lane = me // 4, me % 4
    half = me // 8
    inner = (plane == 1) | (plane == 2)
    beside = (plane + 1 - 2 * (plane % 2)) * 4 + lane
    across = (3 - plane) * 4 + lane
    span = span_hbm.shape[0]
    prefix = prefix_hbm.shape[0]
    keys = prefix + span
    block = span // 4
    pages_dev = span // PAGE

    span_copy = pltpu.make_async_copy(span_hbm, kv.at[pl.ds(prefix, span)], span_sem)
    loads = []
    for g in range(KV_HEADS):
        wide = pl.ds(g * GROUP_WIDTH, GROUP_WIDTH)
        k_cols = pl.ds(g * HEAD_DIM, HEAD_DIM)
        v_cols = pl.ds(KEY_WIDTH + g * HEAD_DIM, HEAD_DIM)
        loads.append([
            pltpu.make_async_copy(q_hbm.at[:, wide], q.at[:, wide], q_sem.at[g]),
            pltpu.make_async_copy(
                prefix_hbm.at[:, k_cols], kv.at[pl.ds(0, prefix), k_cols], k_sem.at[g]),
            pltpu.make_async_copy(
                prefix_hbm.at[:, v_cols], kv.at[pl.ds(0, prefix), v_cols], v_sem.at[g]),
        ])
    span_copy.start()
    for group in loads:
        for copy in group:
            copy.start()

    barrier = pltpu.get_barrier_semaphore()

    @pl.loop(1, n)
    def _(k):
        pl.semaphore_signal(
            barrier, inc=1, device_id={"inst": lax.rem(me + k, n)}, device_id_type=MESH)

    count = counts[me]
    length = lengths[me]
    row = lax.broadcasted_iota(jnp.int32, (span, keys), 0)
    column = lax.broadcasted_iota(jnp.int32, (span, keys), 1)
    limit = jnp.where(column < prefix, length, row + (prefix + 1))
    bias[...] = jnp.where(column < limit, 0.0, -1e30)
    pl.semaphore_wait(barrier, n - 1)

    def remote(src, dst, send, recv, peer):
        return pltpu.make_async_remote_copy(
            src_ref=src, dst_ref=dst, send_sem=send, recv_sem=recv,
            device_id={"inst": peer}, device_id_type=MESH)

    def finish(ref, sem):
        pltpu.make_async_copy(ref, ref, sem).wait()

    own_pages = page_held.at[pl.ds(me * pages_dev, pages_dev)]

    @pl.loop(1, n)
    def _(k):
        peer = lax.rem(me + k, n)
        remote(new_hbm.at[:, :, pl.ds(pl.multiple_of(peer * 128, 128), 128)], own_pages,
               page_sem.at[0], page_sem.at[1], peer).start()

    pltpu.make_async_copy(
        new_hbm.at[:, :, pl.ds(pl.multiple_of(me * 128, 128), 128)], own_pages,
        page_sem.at[1]).start()

    scale = math.log2(math.e) / math.sqrt(HEAD_DIM)
    live = lax.broadcasted_iota(jnp.int32, (span, HEAD_DIM), 0) < count

    def attend(g):
        for copy in loads[g]:
            copy.wait()

        @pl.loop(0, 4)
        def _(pair):
            first = pl.multiple_of(g * GROUP_WIDTH + pair * 256, 256)
            two = q[:, pl.ds(first, 256)]
            rows = jnp.concatenate([two[:, :HEAD_DIM], two[:, HEAD_DIM:]], axis=0)
            key = kv[:, g * HEAD_DIM:(g + 1) * HEAD_DIM]
            value = kv[:, KEY_WIDTH + g * HEAD_DIM:KEY_WIDTH + (g + 1) * HEAD_DIM]
            scores = lax.dot_general(
                rows, key, (((1,), (1,)), ((), ())), preferred_element_type=jnp.float32)
            scores = scores.reshape(2, span, keys) * scale + bias[...][None]
            top = jnp.max(scores, axis=2, keepdims=True)
            shifted = jnp.exp2(scores - top)
            total = jnp.sum(shifted, axis=2, keepdims=True)
            mixed = jnp.dot(
                shifted.reshape(2 * span, keys).astype(jnp.bfloat16), value,
                preferred_element_type=jnp.float32)
            mixed = mixed.reshape(2, span, HEAD_DIM) / total
            mixed = jnp.where(live[None], mixed, 0.0).astype(jnp.bfloat16)
            for h in range(2):
                at = pl.multiple_of(pair * 256 + h * HEAD_DIM, HEAD_DIM)
                for r in range(4):
                    stage[g, r, :, pl.ds(at, HEAD_DIM)] = mixed[h, r * block:(r + 1) * block]

    def spread(g):
        @pl.loop(1, 4)
        def _(k):
            to = lax.rem(lane + k, 4)
            remote(stage.at[g, to], near[g].at[lane], sent.at[0], near_sem.at[g],
                   plane * 4 + to).start()

        pltpu.make_async_copy(stage.at[g, lane], near[g].at[lane], near_sem.at[g]).start()

    def to_inner(g):
        finish(near[g].at[pl.ds(0, 4)], near_sem.at[g])

        @pl.when(jnp.logical_not(inner))
        def _():
            remote(near[g].at[pl.ds(0, 4)], near[g].at[pl.ds(4, 4)], sent.at[1],
                   next_sem.at[g], beside).start()

    def near_place(source):
        other = jnp.where(inner & (source // 4 != plane), 4, 0)
        return other + source % 4

    def cross(g):
        @pl.when(inner)
        def _():
            finish(near[g].at[pl.ds(4, 4)], next_sem.at[g])

            @pl.loop(0, most)
            def _(r):
                middle[g, r] = near[g][near_place(plan[half * 8 + r])]

            remote(middle.at[g], far[g].at[pl.ds(0, most)], sent.at[2], far_sem.at[g],
                   across).start()

    def pick(g, dest, k):
        source = source_of[dest]
        from_far = jnp.where(inner, source // 8 != half, source // 4 != plane)
        far_place = jnp.where(inner, plan[16 + source], k)
        return lax.select_n(from_far, near[g][near_place(source)], far[g][far_place])

    def to_outer(g):
        @pl.when(inner)
        def _():
            finish(far[g].at[pl.ds(0, most)], far_sem.at[g])

            @pl.loop(0, 4)
            def _(k):
                outward[g, k] = pick(g, beside - lane + k, k)

            remote(outward.at[g], far[g].at[pl.ds(0, 4)], sent.at[3], far_sem.at[g],
                   beside).start()

    def deliver(g):
        @pl.when(jnp.logical_not(inner))
        def _():
            finish(far[g].at[pl.ds(0, 4)], far_sem.at[g])

        place = out_hbm.at[
            pl.ds(pl.multiple_of(lane * block, block), block),
            pl.ds(g * GROUP_WIDTH, GROUP_WIDTH),
        ]

        @pl.loop(0, 4)
        def _(k):
            to = lax.rem(lane + k, 4)
            final[g, to] = pick(g, plane * 4 + to, to)

            @pl.when(k > 0)
            def _():
                remote(final.at[g, to], place, sent.at[4], sent.at[5], plane * 4 + to).start()

            @pl.when(k == 0)
            def _():
                pltpu.make_async_copy(final.at[g, to], place, sent.at[5]).start()

    def send_pages():
        finish(page_held, page_sem.at[1])
        place = pages_hbm.at[:, :, pl.ds(pl.multiple_of(me * 128, 128), 128)]

        @pl.loop(0, n)
        def _(k):
            peer = lax.rem(me + k, n)
            for slot in range(pages_dev):
                at = peer * pages_dev + slot
                page_stage[at] = page_held[page_source[at]]

            src = page_stage.at[pl.ds(peer * pages_dev, pages_dev)]

            @pl.when(k > 0)
            def _():
                remote(src, place, page_sem.at[2], page_sem.at[3], peer).start()

            @pl.when(k == 0)
            def _():
                pltpu.make_async_copy(src, place, page_sem.at[3]).start()

    span_copy.wait()
    steps = [(attend, 0), (spread, 0), (to_inner, 1), (cross, 2), (to_outer, 4), (deliver, 6)]
    for t in range(KV_HEADS + 6):
        for step, lag in steps:
            if 0 <= t - lag < KV_HEADS:
                step(t - lag)
        if t == 3:
            send_pages()

    finish(stage.at[:, pl.ds(0, 3)], sent.at[0])

    @pl.when(inner)
    def _():
        finish(middle, sent.at[2])
        finish(outward, sent.at[3])

    @pl.when(jnp.logical_not(inner))
    def _():
        finish(stage, sent.at[1])

    finish(final.at[:, pl.ds(0, 3)], sent.at[4])
    finish(out_hbm, sent.at[5])
    finish(page_held.at[pl.ds(0, (n - 1) * pages_dev)], page_sem.at[0])
    finish(page_stage.at[pl.ds(0, (n - 1) * pages_dev)], page_sem.at[2])
    finish(pages_hbm, page_sem.at[3])


def line_call(n, most, number, small, big):
    span, width = big[0].shape
    prefix, kv_width = big[2].shape
    block = span // 4
    dma = pltpu.SemaphoreType.DMA
    bf16 = jnp.bfloat16
    piece = (block, GROUP_WIDTH)
    pages = big[3].shape[0] * n
    return pl.pallas_call(
        functools.partial(line_kernel, n, most),
        out_shape=[
            jax.ShapeDtypeStruct((span, width), bf16),
            jax.ShapeDtypeStruct(big[3].shape, bf16),
        ],
        in_specs=[pl.BlockSpec(memory_space=pltpu.SMEM)] * len(small)
        + [pl.BlockSpec(memory_space=pl.ANY)] * len(big),
        out_specs=[pl.BlockSpec(memory_space=pl.ANY)] * 2,
        scratch_shapes=[
            pltpu.VMEM((span, width), bf16),
            pltpu.VMEM((prefix + span, kv_width), bf16),
            pltpu.VMEM((span, prefix + span), jnp.float32),
            pltpu.VMEM((KV_HEADS, 4) + piece, bf16),
            pltpu.VMEM((KV_HEADS, most) + piece, bf16),
            pltpu.VMEM((KV_HEADS, 4) + piece, bf16),
            pltpu.VMEM((KV_HEADS, 4) + piece, bf16),
            pltpu.VMEM((pages, PAGE, 128), bf16),
            pltpu.VMEM((pages, PAGE, 128), bf16),
        ]
        + [pltpu.VMEM((8,) + piece, bf16) for _ in range(KV_HEADS)]
        + [pltpu.VMEM((max(most, 4),) + piece, bf16) for _ in range(KV_HEADS)]
        + [
            dma((KV_HEADS,)), dma((KV_HEADS,)), dma((KV_HEADS,)), dma(()),
            dma((KV_HEADS,)), dma((KV_HEADS,)), dma((KV_HEADS,)), dma((4,)), dma((6,)),
        ],
        compiler_params=pltpu.CompilerParams(
            collective_id=number, has_side_effects=True, vmem_limit_bytes=48 * 1024 * 1024),
    )(*small, *big)


def by_lines(queries, span_kv, prefix_kv, span_counts, prefix_lengths, move_to, page_slot):
    n = 16
    span, kv_width = span_kv.shape
    index = jnp.arange(n, dtype=jnp.int32)
    leaves = index // 8 != move_to // 8
    same_half = index[:, None] // 8 == index[None, :] // 8
    earlier = same_half & (index[None, :] < index[:, None]) & leaves[None, :]
    rank = jnp.where(leaves, jnp.sum(earlier.astype(jnp.int32), axis=1), 0)
    place = jnp.where(leaves, rank + index // 8 * 8, -1)
    order = jnp.sum(jnp.where(place[None, :] == index[:, None], index[None, :], 0), axis=1)
    most = jnp.sum(leaves.astype(jnp.int32)) // 2
    groups = lax.axis_size("groups")
    for k in range(1, groups):
        ring = [(g, (g + k) % groups) for g in range(groups)]
        most = jnp.maximum(most, lax.ppermute(jnp.sum(leaves.astype(jnp.int32)) // 2, "groups", ring))
    small = [span_counts, prefix_lengths, inverse(move_to), inverse(page_slot),
             jnp.concatenate([order, rank])]
    big = [queries, span_kv, prefix_kv, span_kv.reshape(span // PAGE, PAGE, kv_width)]
    limits = LIMITS
    branches = [
        functools.partial(line_call, n, limit, 1 + i) for i, limit in enumerate(limits)
    ]
    which = sum([(most > limit).astype(jnp.int32) for limit in limits[:-1]])
    return tuple(lax.switch(which, branches, small, big))


def local(n, queries, span_kv, prefix_kv, span_counts, prefix_lengths, move_to, page_slot):
    span, width = queries.shape
    prefix, kv_width = prefix_kv.shape
    if n == 16:
        return by_lines(
            queries, span_kv, prefix_kv, span_counts, prefix_lengths, move_to, page_slot)
    with_pages = n * 128 == kv_width
    chunks = 128 // n
    anywhere = pl.BlockSpec(memory_space=pl.ANY)
    scalars = pl.BlockSpec(memory_space=pltpu.SMEM)
    small = [span_counts, prefix_lengths, inverse(move_to)]
    out_shape = [jax.ShapeDtypeStruct((span, width), jnp.bfloat16)]
    scratch = [
        pltpu.VMEM((span, width), jnp.bfloat16),
        pltpu.VMEM((prefix + span, kv_width), jnp.bfloat16),
        pltpu.VMEM((span, prefix + span), jnp.float32),
        pltpu.VMEM((KV_HEADS, 16, ROWS, COLS), jnp.bfloat16),
        pltpu.VMEM((chunks, n, ROWS, COLS), jnp.bfloat16),
    ] + [pltpu.VMEM((n, ROWS, COLS), jnp.bfloat16) for _ in range(chunks)]
    big = [queries, span_kv, prefix_kv]
    if with_pages:
        small.append(inverse(page_slot))
        big.append(span_kv.reshape(span // PAGE, PAGE, kv_width))
        out_shape.append(jax.ShapeDtypeStruct((span // PAGE, PAGE, kv_width), jnp.bfloat16))
        scratch += [
            pltpu.VMEM((page_slot.shape[0], PAGE, 128), jnp.bfloat16),
            pltpu.VMEM((page_slot.shape[0], PAGE, 128), jnp.bfloat16),
        ]
    dma = pltpu.SemaphoreType.DMA
    scratch += [
        dma((KV_HEADS,)), dma((KV_HEADS,)), dma((KV_HEADS,)), dma(()),
        dma((1,)), dma((chunks,)), dma((1,)), dma((1,)),
    ]
    if with_pages:
        scratch.append(dma((4,)))
    outs = pl.pallas_call(
        functools.partial(kernel, n, with_pages),
        out_shape=out_shape,
        in_specs=[scalars] * len(small) + [anywhere] * len(big),
        out_specs=[anywhere] * len(out_shape),
        scratch_shapes=scratch,
        compiler_params=pltpu.CompilerParams(
            collective_id=0, has_side_effects=True, vmem_limit_bytes=48 * 1024 * 1024),
    )(*small, *big)
    if with_pages:
        return outs[0], outs[1]
    return outs[0], move_pages(span_kv, page_slot, n)


def solution(mesh):
    placed = (
        P(("groups", "inst"), None),
        P(("groups", "inst"), None),
        P(("groups", "inst"), None),
        P("groups"),
        P("groups"),
        P("groups"),
        P("groups"),
    )
    return jax.shard_map(
        functools.partial(local, mesh.shape["inst"]),
        mesh=mesh,
        in_specs=placed,
        out_specs=(P(("groups", "inst"), None), P(("groups", "inst"), None, None)),
        check_vma=False,
    )
```

```python
import functools
import math

import jax
import jax.numpy as jnp
from jax import lax
from jax.experimental import pallas as pl
from jax.experimental.pallas import tpu as pltpu
from jax.sharding import PartitionSpec as P

HEADS = 64
KV_HEADS = 8
HEAD_DIM = 128
PAGE = 16
KEY_WIDTH = KV_HEADS * HEAD_DIM
GROUP_WIDTH = HEADS // KV_HEADS * HEAD_DIM
ROWS = 16
COLS = 512
LIMITS = (4, 5, 8)
STEPS = 16
STEP_WIDTH = HEADS * HEAD_DIM // STEPS
MESH = pl.DeviceIdType.MESH


def kernel(n, with_pages, *refs):
    if with_pages:
        (counts, lengths, source_of, page_source, q_hbm, span_hbm, prefix_hbm, new_hbm,
         out_hbm, pages_hbm, q, kv, bias, stage, relay, *rest) = refs
        chunks = 128 // n
        held = rest[:chunks]
        (page_stage, page_held, q_sem, k_sem, v_sem, span_sem, send_sem, held_sem, relay_sem,
         out_sem, page_sem) = rest[chunks:]
    else:
        (counts, lengths, source_of, q_hbm, span_hbm, prefix_hbm,
         out_hbm, q, kv, bias, stage, relay, *rest) = refs
        chunks = 128 // n
        held = rest[:chunks]
        q_sem, k_sem, v_sem, span_sem, send_sem, held_sem, relay_sem, out_sem = rest[chunks:]
    me = lax.axis_index("inst")
    span = span_hbm.shape[0]
    prefix = prefix_hbm.shape[0]
    keys = prefix + span

    span_copies = [
        pltpu.make_async_copy(span_hbm, kv.at[pl.ds(prefix, span)], span_sem)
    ]
    loads = []
    for g in range(KV_HEADS):
        wide = pl.ds(g * GROUP_WIDTH, GROUP_WIDTH)
        k_cols = pl.ds(g * HEAD_DIM, HEAD_DIM)
        v_cols = pl.ds(KEY_WIDTH + g * HEAD_DIM, HEAD_DIM)
        loads.append([
            pltpu.make_async_copy(q_hbm.at[:, wide], q.at[:, wide], q_sem.at[g]),
            pltpu.make_async_copy(
                prefix_hbm.at[:, k_cols], kv.at[pl.ds(0, prefix), k_cols], k_sem.at[g]),
            pltpu.make_async_copy(
                prefix_hbm.at[:, v_cols], kv.at[pl.ds(0, prefix), v_cols], v_sem.at[g]),
        ])
    span_copies[0].start()
    for group in loads:
        for copy in group:
            copy.start()

    barrier = pltpu.get_barrier_semaphore()

    @pl.loop(1, n)
    def _(k):
        pl.semaphore_signal(
            barrier, inc=1, device_id={"inst": lax.rem(me + k, n)}, device_id_type=MESH)

    count = counts[me]
    length = lengths[me]
    row = lax.broadcasted_iota(jnp.int32, (span, keys), 0)
    column = lax.broadcasted_iota(jnp.int32, (span, keys), 1)
    limit = jnp.where(column < prefix, length, row + (prefix + 1))
    bias[...] = jnp.where(column < limit, 0.0, -1e30)
    pl.semaphore_wait(barrier, n - 1)

    if with_pages:
        pages_dev = span // PAGE

        @pl.loop(1, n)
        def _(k):
            peer = lax.rem(me + k, n)
            pltpu.make_async_remote_copy(
                src_ref=new_hbm.at[:, :, pl.ds(pl.multiple_of(peer * 128, 128), 128)],
                dst_ref=page_held.at[pl.ds(me * pages_dev, pages_dev)],
                send_sem=page_sem.at[0],
                recv_sem=page_sem.at[1],
                device_id={"inst": peer},
                device_id_type=MESH,
            ).start()

        pltpu.make_async_copy(
            new_hbm.at[:, :, pl.ds(pl.multiple_of(me * 128, 128), 128)],
            page_held.at[pl.ds(me * pages_dev, pages_dev)],
            page_sem.at[1],
        ).start()

    scale = math.log2(math.e) / math.sqrt(HEAD_DIM)
    live = lax.broadcasted_iota(jnp.int32, (span, HEAD_DIM), 0) < count

    def attend(g):
        @pl.loop(0, 4)
        def _(pair):
            first = pl.multiple_of(g * GROUP_WIDTH + pair * 256, 256)
            two = q[:, pl.ds(first, 256)]
            rows = jnp.concatenate([two[:, :HEAD_DIM], two[:, HEAD_DIM:]], axis=0)
            key = kv[:, g * HEAD_DIM:(g + 1) * HEAD_DIM]
            value = kv[:, KEY_WIDTH + g * HEAD_DIM:KEY_WIDTH + (g + 1) * HEAD_DIM]
            scores = lax.dot_general(
                rows, key, (((1,), (1,)), ((), ())), preferred_element_type=jnp.float32)
            scores = scores.reshape(2, span, keys) * scale + bias[...][None]
            top = jnp.max(scores, axis=2, keepdims=True)
            shifted = jnp.exp2(scores - top)
            total = jnp.sum(shifted, axis=2, keepdims=True)
            mixed = jnp.dot(
                shifted.reshape(2 * span, keys).astype(jnp.bfloat16), value,
                preferred_element_type=jnp.float32)
            mixed = mixed.reshape(2, span, HEAD_DIM) / total
            mixed = jnp.where(live[None], mixed, 0.0).astype(jnp.bfloat16)
            half = pair // 2
            for h in range(2):
                at = pl.multiple_of((pair % 2) * 256 + h * HEAD_DIM, HEAD_DIM)
                for r in range(8):
                    stage[g, half * 8 + r, :, pl.ds(at, HEAD_DIM)] = (
                        mixed[h, r * ROWS:(r + 1) * ROWS])

    def spread(g):
        c = g * 16 // n

        @pl.loop(0, 16)
        def _(k):
            j = lax.rem(me + k, 16)
            target = (g * 16) % n + j

            @pl.when(target != me)
            def _():
                pltpu.make_async_remote_copy(
                    src_ref=stage.at[g, j],
                    dst_ref=held[c].at[me],
                    send_sem=send_sem.at[0],
                    recv_sem=held_sem.at[c],
                    device_id={"inst": target},
                    device_id_type=MESH,
                ).start()

            @pl.when(target == me)
            def _():
                pltpu.make_async_copy(stage.at[g, j], held[c].at[me], held_sem.at[c]).start()

    def send_on(c):
        pltpu.make_async_copy(held[c], held[c], held_sem.at[c]).wait()
        piece = c * n + me
        g = piece // 16
        j = piece % 16
        place = out_hbm.at[
            pl.ds(pl.multiple_of((j % 8) * ROWS, ROWS), ROWS),
            pl.ds(pl.multiple_of(g * GROUP_WIDTH + (j // 8) * COLS, COLS), COLS),
        ]

        @pl.loop(0, n)
        def _(k):
            peer = lax.rem(me + k, n)
            relay[c, peer] = held[c][source_of[peer]]

            @pl.when(k > 0)
            def _():
                pltpu.make_async_remote_copy(
                    src_ref=relay.at[c, peer],
                    dst_ref=place,
                    send_sem=relay_sem.at[0],
                    recv_sem=out_sem.at[0],
                    device_id={"inst": peer},
                    device_id_type=MESH,
                ).start()

            @pl.when(k == 0)
            def _():
                pltpu.make_async_copy(relay.at[c, peer], place, out_sem.at[0]).start()

    def send_pages():
        pltpu.make_async_copy(page_held, page_held, page_sem.at[1]).wait()
        place = pages_hbm.at[:, :, pl.ds(pl.multiple_of(me * 128, 128), 128)]

        @pl.loop(0, n)
        def _(k):
            peer = lax.rem(me + k, n)
            for slot in range(pages_dev):
                at = peer * pages_dev + slot
                page_stage[at] = page_held[page_source[at]]

            src = page_stage.at[pl.ds(peer * pages_dev, pages_dev)]

            @pl.when(k > 0)
            def _():
                pltpu.make_async_remote_copy(
                    src_ref=src,
                    dst_ref=place,
                    send_sem=page_sem.at[2],
                    recv_sem=page_sem.at[3],
                    device_id={"inst": peer},
                    device_id_type=MESH,
                ).start()

            @pl.when(k == 0)
            def _():
                pltpu.make_async_copy(src, place, page_sem.at[3]).start()

    lag = 3
    span_copies[0].wait()
    sent = 0
    for g in range(KV_HEADS):
        for copy in loads[g]:
            copy.wait()
        attend(g)
        spread(g)
        if with_pages and g == 3:
            send_pages()
        if n == 16 and g >= lag:
            send_on(sent)
            sent += 1
    for c in range(sent, chunks):
        send_on(c)

    away = 128 - chunks
    flat = stage.at[:, pl.ds(0, 15)]
    if n == 16:
        pltpu.make_async_copy(flat, flat, send_sem.at[0]).wait()
        flat = relay.at[:, pl.ds(0, n - 1)]
        pltpu.make_async_copy(flat, flat, relay_sem.at[0]).wait()
    else:
        flat = relay.at[0, pl.ds(0, away)]
        pltpu.make_async_copy(flat, flat, send_sem.at[0]).wait()
        pltpu.make_async_copy(flat, flat, relay_sem.at[0]).wait()
    pltpu.make_async_copy(out_hbm, out_hbm, out_sem.at[0]).wait()
    if with_pages:
        some = page_held.at[pl.ds(0, (n - 1) * pages_dev)]
        pltpu.make_async_copy(some, some, page_sem.at[0]).wait()
        some = page_stage.at[pl.ds(0, (n - 1) * pages_dev)]
        pltpu.make_async_copy(some, some, page_sem.at[2]).wait()
        pltpu.make_async_copy(pages_hbm, pages_hbm, page_sem.at[3]).wait()


def inverse(order):
    index = jnp.arange(order.shape[0], dtype=jnp.int32)
    return jnp.sum(jnp.where(order[None, :] == index[:, None], index[None, :], 0), axis=1)


def move_pages(span_kv, page_slot, inst_count):
    pages_here = span_kv.shape[0] // PAGE
    piece_width = PAGE * span_kv.shape[1] // inst_count
    flat_pages = span_kv.reshape(pages_here, inst_count, piece_width)
    spread_pages = lax.all_to_all(flat_pages, "inst", split_axis=1, concat_axis=0, tiled=True)
    ordered_pages = jnp.take(spread_pages, inverse(page_slot), axis=0)
    arrived = lax.all_to_all(ordered_pages, "inst", split_axis=0, concat_axis=1, tiled=True)
    return arrived.reshape(pages_here, PAGE, span_kv.shape[1])


def line_kernel(n, most, counts, lengths, source_of, page_source, plan, q_hbm, span_hbm,
                prefix_hbm, new_hbm, out_hbm, pages_hbm, q, kv, bias, stage, middle, outward,
                final, page_stage, page_held, *rest):
    near, far = rest[:STEPS], rest[STEPS:2 * STEPS]
    (q_sem, k_sem, v_sem, span_sem, near_sem, next_sem, far_sem, page_sem,
     sent) = rest[2 * STEPS:]
    me = lax.axis_index("inst")
    plane, lane = me // 4, me % 4
    half = me // 8
    inner = (plane == 1) | (plane == 2)
    beside = (plane + 1 - 2 * (plane % 2)) * 4 + lane
    across = (3 - plane) * 4 + lane
    span = span_hbm.shape[0]
    prefix = prefix_hbm.shape[0]
    keys = prefix + span
    block = span // 4
    pages_dev = span // PAGE

    span_copy = pltpu.make_async_copy(span_hbm, kv.at[pl.ds(prefix, span)], span_sem)
    loads = []
    for g in range(KV_HEADS):
        wide = pl.ds(g * GROUP_WIDTH, GROUP_WIDTH)
        k_cols = pl.ds(g * HEAD_DIM, HEAD_DIM)
        v_cols = pl.ds(KEY_WIDTH + g * HEAD_DIM, HEAD_DIM)
        loads.append([
            pltpu.make_async_copy(q_hbm.at[:, wide], q.at[:, wide], q_sem.at[g]),
            pltpu.make_async_copy(
                prefix_hbm.at[:, k_cols], kv.at[pl.ds(0, prefix), k_cols], k_sem.at[g]),
            pltpu.make_async_copy(
                prefix_hbm.at[:, v_cols], kv.at[pl.ds(0, prefix), v_cols], v_sem.at[g]),
        ])
    span_copy.start()
    for group in loads:
        for copy in group:
            copy.start()

    barrier = pltpu.get_barrier_semaphore()

    @pl.loop(1, n)
    def _(k):
        pl.semaphore_signal(
            barrier, inc=1, device_id={"inst": lax.rem(me + k, n)}, device_id_type=MESH)

    count = counts[me]
    length = lengths[me]
    row = lax.broadcasted_iota(jnp.int32, (span, keys), 0)
    column = lax.broadcasted_iota(jnp.int32, (span, keys), 1)
    limit = jnp.where(column < prefix, length, row + (prefix + 1))
    bias[...] = jnp.where(column < limit, 0.0, -1e30)
    pl.semaphore_wait(barrier, n - 1)

    def remote(src, dst, send, recv, peer):
        return pltpu.make_async_remote_copy(
            src_ref=src, dst_ref=dst, send_sem=send, recv_sem=recv,
            device_id={"inst": peer}, device_id_type=MESH)

    def finish(ref, sem):
        pltpu.make_async_copy(ref, ref, sem).wait()

    own_pages = page_held.at[pl.ds(me * pages_dev, pages_dev)]

    @pl.loop(1, n)
    def _(k):
        peer = lax.rem(me + k, n)
        remote(new_hbm.at[:, :, pl.ds(pl.multiple_of(peer * 128, 128), 128)], own_pages,
               page_sem.at[0], page_sem.at[1], peer).start()

    pltpu.make_async_copy(
        new_hbm.at[:, :, pl.ds(pl.multiple_of(me * 128, 128), 128)], own_pages,
        page_sem.at[1]).start()

    scale = math.log2(math.e) / math.sqrt(HEAD_DIM)
    live = lax.broadcasted_iota(jnp.int32, (span, HEAD_DIM), 0) < count

    def attend(c):
        g = c * KV_HEADS // STEPS
        if c * KV_HEADS % STEPS == 0:
            for copy in loads[g]:
                copy.wait()

        @pl.loop(0, STEP_WIDTH // 256)
        def _(pair):
            first = pl.multiple_of(c * STEP_WIDTH + pair * 256, 256)
            two = q[:, pl.ds(first, 256)]
            rows = jnp.concatenate([two[:, :HEAD_DIM], two[:, HEAD_DIM:]], axis=0)
            key = kv[:, g * HEAD_DIM:(g + 1) * HEAD_DIM]
            value = kv[:, KEY_WIDTH + g * HEAD_DIM:KEY_WIDTH + (g + 1) * HEAD_DIM]
            scores = lax.dot_general(
                rows, key, (((1,), (1,)), ((), ())), preferred_element_type=jnp.float32)
            scores = scores.reshape(2, span, keys) * scale + bias[...][None]
            top = jnp.max(scores, axis=2, keepdims=True)
            shifted = jnp.exp2(scores - top)
            total = jnp.sum(shifted, axis=2, keepdims=True)
            mixed = jnp.dot(
                shifted.reshape(2 * span, keys).astype(jnp.bfloat16), value,
                preferred_element_type=jnp.float32)
            mixed = mixed.reshape(2, span, HEAD_DIM) / total
            mixed = jnp.where(live[None], mixed, 0.0).astype(jnp.bfloat16)
            for h in range(2):
                at = pl.multiple_of(pair * 256 + h * HEAD_DIM, HEAD_DIM)
                for r in range(4):
                    stage[c, r, :, pl.ds(at, HEAD_DIM)] = mixed[h, r * block:(r + 1) * block]

    def spread(g):
        @pl.loop(1, 4)
        def _(k):
            to = lax.rem(lane + k, 4)
            remote(stage.at[g, to], near[g].at[lane], sent.at[0], near_sem.at[g],
                   plane * 4 + to).start()

        pltpu.make_async_copy(stage.at[g, lane], near[g].at[lane], near_sem.at[g]).start()

    def to_inner(g):
        finish(near[g].at[pl.ds(0, 4)], near_sem.at[g])

        @pl.when(jnp.logical_not(inner))
        def _():
            remote(near[g].at[pl.ds(0, 4)], near[g].at[pl.ds(4, 4)], sent.at[1],
                   next_sem.at[g], beside).start()

    def near_place(source):
        other = jnp.where(inner & (source // 4 != plane), 4, 0)
        return other + source % 4

    def cross(g):
        @pl.when(inner)
        def _():
            finish(near[g].at[pl.ds(4, 4)], next_sem.at[g])

            @pl.loop(0, most)
            def _(r):
                middle[g, r] = near[g][near_place(plan[half * 8 + r])]

            remote(middle.at[g], far[g].at[pl.ds(0, most)], sent.at[2], far_sem.at[g],
                   across).start()

    def pick(g, dest, k):
        source = source_of[dest]
        from_far = jnp.where(inner, source // 8 != half, source // 4 != plane)
        far_place = jnp.where(inner, plan[16 + source], k)
        return lax.select_n(from_far, near[g][near_place(source)], far[g][far_place])

    def to_outer(g):
        @pl.when(inner)
        def _():
            finish(far[g].at[pl.ds(0, most)], far_sem.at[g])

            @pl.loop(0, 4)
            def _(k):
                outward[g, k] = pick(g, beside - lane + k, k)

            remote(outward.at[g], far[g].at[pl.ds(0, 4)], sent.at[3], far_sem.at[g],
                   beside).start()

    def deliver(g):
        @pl.when(jnp.logical_not(inner))
        def _():
            finish(far[g].at[pl.ds(0, 4)], far_sem.at[g])

        place = out_hbm.at[
            pl.ds(pl.multiple_of(lane * block, block), block),
            pl.ds(g * STEP_WIDTH, STEP_WIDTH),
        ]

        @pl.loop(0, 4)
        def _(k):
            to = lax.rem(lane + k, 4)
            final[g, to] = pick(g, plane * 4 + to, to)

            @pl.when(k > 0)
            def _():
                remote(final.at[g, to], place, sent.at[4], sent.at[5], plane * 4 + to).start()

            @pl.when(k == 0)
            def _():
                pltpu.make_async_copy(final.at[g, to], place, sent.at[5]).start()

    def send_pages():
        finish(page_held, page_sem.at[1])
        place = pages_hbm.at[:, :, pl.ds(pl.multiple_of(me * 128, 128), 128)]

        @pl.loop(0, n)
        def _(k):
            peer = lax.rem(me + k, n)
            for slot in range(pages_dev):
                at = peer * pages_dev + slot
                page_stage[at] = page_held[page_source[at]]

            src = page_stage.at[pl.ds(peer * pages_dev, pages_dev)]

            @pl.when(k > 0)
            def _():
                remote(src, place, page_sem.at[2], page_sem.at[3], peer).start()

            @pl.when(k == 0)
            def _():
                pltpu.make_async_copy(src, place, page_sem.at[3]).start()

    span_copy.wait()
    steps = [(attend, 0), (spread, 0), (to_inner, 1), (cross, 3), (to_outer, 6), (deliver, 8)]
    for t in range(STEPS + 8):
        for step, lag in steps:
            if 0 <= t - lag < STEPS:
                step(t - lag)
        if t == 5:
            send_pages()

    finish(stage.at[:, pl.ds(0, 3)], sent.at[0])

    @pl.when(inner)
    def _():
        finish(middle, sent.at[2])
        finish(outward, sent.at[3])

    @pl.when(jnp.logical_not(inner))
    def _():
        finish(stage, sent.at[1])

    finish(final.at[:, pl.ds(0, 3)], sent.at[4])
    finish(out_hbm, sent.at[5])
    finish(page_held.at[pl.ds(0, (n - 1) * pages_dev)], page_sem.at[0])
    finish(page_stage.at[pl.ds(0, (n - 1) * pages_dev)], page_sem.at[2])
    finish(pages_hbm, page_sem.at[3])


def line_call(n, most, number, small, big):
    span, width = big[0].shape
    prefix, kv_width = big[2].shape
    block = span // 4
    dma = pltpu.SemaphoreType.DMA
    bf16 = jnp.bfloat16
    piece = (block, STEP_WIDTH)
    pages = big[3].shape[0] * n
    return pl.pallas_call(
        functools.partial(line_kernel, n, most),
        out_shape=[
            jax.ShapeDtypeStruct((span, width), bf16),
            jax.ShapeDtypeStruct(big[3].shape, bf16),
        ],
        in_specs=[pl.BlockSpec(memory_space=pltpu.SMEM)] * len(small)
        + [pl.BlockSpec(memory_space=pl.ANY)] * len(big),
        out_specs=[pl.BlockSpec(memory_space=pl.ANY)] * 2,
        scratch_shapes=[
            pltpu.VMEM((span, width), bf16),
            pltpu.VMEM((prefix + span, kv_width), bf16),
            pltpu.VMEM((span, prefix + span), jnp.float32),
            pltpu.VMEM((STEPS, 4) + piece, bf16),
            pltpu.VMEM((STEPS, most) + piece, bf16),
            pltpu.VMEM((STEPS, 4) + piece, bf16),
            pltpu.VMEM((STEPS, 4) + piece, bf16),
            pltpu.VMEM((pages, PAGE, 128), bf16),
            pltpu.VMEM((pages, PAGE, 128), bf16),
        ]
        + [pltpu.VMEM((8,) + piece, bf16) for _ in range(STEPS)]
        + [pltpu.VMEM((max(most, 4),) + piece, bf16) for _ in range(STEPS)]
        + [
            dma((KV_HEADS,)), dma((KV_HEADS,)), dma((KV_HEADS,)), dma(()),
            dma((STEPS,)), dma((STEPS,)), dma((STEPS,)), dma((4,)), dma((6,)),
        ],
        compiler_params=pltpu.CompilerParams(
            collective_id=number, has_side_effects=True, vmem_limit_bytes=48 * 1024 * 1024),
    )(*small, *big)


def by_lines(queries, span_kv, prefix_kv, span_counts, prefix_lengths, move_to, page_slot):
    n = 16
    span, kv_width = span_kv.shape
    index = jnp.arange(n, dtype=jnp.int32)
    leaves = index // 8 != move_to // 8
    same_half = index[:, None] // 8 == index[None, :] // 8
    earlier = same_half & (index[None, :] < index[:, None]) & leaves[None, :]
    rank = jnp.where(leaves, jnp.sum(earlier.astype(jnp.int32), axis=1), 0)
    place = jnp.where(leaves, rank + index // 8 * 8, -1)
    order = jnp.sum(jnp.where(place[None, :] == index[:, None], index[None, :], 0), axis=1)
    most = jnp.sum(leaves.astype(jnp.int32)) // 2
    groups = lax.axis_size("groups")
    for k in range(1, groups):
        ring = [(g, (g + k) % groups) for g in range(groups)]
        most = jnp.maximum(most, lax.ppermute(jnp.sum(leaves.astype(jnp.int32)) // 2, "groups", ring))
    small = [span_counts, prefix_lengths, inverse(move_to), inverse(page_slot),
             jnp.concatenate([order, rank])]
    big = [queries, span_kv, prefix_kv, span_kv.reshape(span // PAGE, PAGE, kv_width)]
    limits = LIMITS
    branches = [
        functools.partial(line_call, n, limit, 1 + i) for i, limit in enumerate(limits)
    ]
    which = sum([(most > limit).astype(jnp.int32) for limit in limits[:-1]])
    return tuple(lax.switch(which, branches, small, big))


def local(n, queries, span_kv, prefix_kv, span_counts, prefix_lengths, move_to, page_slot):
    span, width = queries.shape
    prefix, kv_width = prefix_kv.shape
    if n == 16:
        return by_lines(
            queries, span_kv, prefix_kv, span_counts, prefix_lengths, move_to, page_slot)
    with_pages = n * 128 == kv_width
    chunks = 128 // n
    anywhere = pl.BlockSpec(memory_space=pl.ANY)
    scalars = pl.BlockSpec(memory_space=pltpu.SMEM)
    small = [span_counts, prefix_lengths, inverse(move_to)]
    out_shape = [jax.ShapeDtypeStruct((span, width), jnp.bfloat16)]
    scratch = [
        pltpu.VMEM((span, width), jnp.bfloat16),
        pltpu.VMEM((prefix + span, kv_width), jnp.bfloat16),
        pltpu.VMEM((span, prefix + span), jnp.float32),
        pltpu.VMEM((KV_HEADS, 16, ROWS, COLS), jnp.bfloat16),
        pltpu.VMEM((chunks, n, ROWS, COLS), jnp.bfloat16),
    ] + [pltpu.VMEM((n, ROWS, COLS), jnp.bfloat16) for _ in range(chunks)]
    big = [queries, span_kv, prefix_kv]
    if with_pages:
        small.append(inverse(page_slot))
        big.append(span_kv.reshape(span // PAGE, PAGE, kv_width))
        out_shape.append(jax.ShapeDtypeStruct((span // PAGE, PAGE, kv_width), jnp.bfloat16))
        scratch += [
            pltpu.VMEM((page_slot.shape[0], PAGE, 128), jnp.bfloat16),
            pltpu.VMEM((page_slot.shape[0], PAGE, 128), jnp.bfloat16),
        ]
    dma = pltpu.SemaphoreType.DMA
    scratch += [
        dma((KV_HEADS,)), dma((KV_HEADS,)), dma((KV_HEADS,)), dma(()),
        dma((1,)), dma((chunks,)), dma((1,)), dma((1,)),
    ]
    if with_pages:
        scratch.append(dma((4,)))
    outs = pl.pallas_call(
        functools.partial(kernel, n, with_pages),
        out_shape=out_shape,
        in_specs=[scalars] * len(small) + [anywhere] * len(big),
        out_specs=[anywhere] * len(out_shape),
        scratch_shapes=scratch,
        compiler_params=pltpu.CompilerParams(
            collective_id=0, has_side_effects=True, vmem_limit_bytes=48 * 1024 * 1024),
    )(*small, *big)
    if with_pages:
        return outs[0], outs[1]
    return outs[0], move_pages(span_kv, page_slot, n)


def solution(mesh):
    placed = (
        P(("groups", "inst"), None),
        P(("groups", "inst"), None),
        P(("groups", "inst"), None),
        P("groups"),
        P("groups"),
        P("groups"),
        P("groups"),
    )
    return jax.shard_map(
        functools.partial(local, mesh.shape["inst"]),
        mesh=mesh,
        in_specs=placed,
        out_specs=(P(("groups", "inst"), None), P(("groups", "inst"), None, None)),
        check_vma=False,
    )
```
